256 devices in a mesh: row: 8 (over y, core), col: 32 (over z, x).
Axes of the slice: x: 4, y: 4, z: 8, core: 2. Of those that a mesh axis runs over, the one named last changes fastest.
Arguments:
- covariance: float32 [8, 2048, 2, 8192], P(None, 'row', None, 'col'), as said below
Outputs:
- factored: float32 [8, 2048, 2, 8192], P(None, 'row', None, 'col')
Inputs may be any that keep to these rules, and one draw needn't show every extreme that they name: `covariance`: symmetric positive definite.
All inputs are finite; a program needn't handle non-finite values.
Results may differ from the reference program's by a relative error of at most 0.0001.
Values sent between devices are 32-bit elements; how exact they have to be, the bound alone decides.
No kernel may reach another device: no remote copies, remote signals or barrier semaphores. Data moves between devices by JAX's collectives and lax.ppermute only.
A program may use at most 64 MiB of HBM per device.

```python
import math
import jax
import jax.numpy as jnp
from jax import lax

N = 16384
NB = 256
PANELS = 3
TROW = 8
TCOL = 2
N_ROW = 8
N_COL = 32


def draw_covariance(key, part):
    key = jax.random.fold_in(key, 11)
    key_locs, key_noise = jax.random.split(key, 2)
    locations = jax.random.uniform(key_locs, (N, 2), jnp.float32)
    delta_x = locations[:, 0][:, None] - locations[:, 0][None, :]
    delta_y = locations[:, 1][:, None] - locations[:, 1][None, :]
    scaled = math.sqrt(3.0) * jnp.sqrt(delta_x * delta_x + delta_y * delta_y) / 0.1
    kernel = (1.0 + scaled) * jnp.exp(-scaled)
    gauss = jax.random.normal(key_noise, (N, N), jnp.float32)
    noise = (gauss + gauss.T) / math.sqrt(2.0 * N)
    full = kernel + noise + 5.0 * jnp.eye(N, dtype=jnp.float32)
    return full.reshape(TROW, N_ROW * NB, TCOL, N_COL * NB)


def setup_inputs(seed: int = 0) -> dict:
    seeds = jax.random.split(jax.random.key(seed), 2)
    covariance = draw_covariance(jax.random.fold_in(seeds[1], 71), 0)
    return dict(covariance=covariance)


def solve_right(factor, panel):
    return lax.linalg.triangular_solve(factor, panel, left_side=False, lower=True, transpose_a=True)

def reference(covariance):
    matrix = covariance.reshape(N, N)
    for panel_index in range(PANELS):
        start_col = panel_index * NB
        end_col = start_col + NB
        factor = jnp.linalg.cholesky(matrix[start_col:end_col, start_col:end_col])
        below_panel = solve_right(factor, matrix[end_col:, start_col:end_col])
        update = jnp.dot(below_panel, below_panel.T, precision=lax.Precision.HIGHEST)
        matrix = matrix.at[end_col:, end_col:].set(matrix[end_col:, end_col:] - update)
        matrix = matrix.at[start_col:end_col, start_col:end_col].set(jnp.tril(factor))
        matrix = matrix.at[end_col:, start_col:end_col].set(below_panel)
        matrix = matrix.at[start_col:end_col, end_col:].set(jnp.float32(0.0))
        matrix = matrix.at[:start_col, start_col:end_col].set(jnp.float32(0.0))
    return matrix.reshape(covariance.shape)
```

```python
import jax
import jax.numpy as jnp
from jax import lax
from jax.sharding import PartitionSpec as P

NB = 256
PANELS = 3
K = PANELS * NB
NY, NX, NZ = 4, 4, 8
HI = lax.Precision.HIGHEST


def row_perm(shift):
    return [(y * 2 + core, ((y + shift) % NY) * 2 + core) for y in range(NY) for core in range(2)]


def x_perm(shift, limit):
    return [(z * NX + x, z * NX + (x + shift) % NX) for z in range(NZ) for x in range(limit)]


def z_perm(step):
    pairs = [(z, z + step) for z in range(0, NZ, 2 * step)]
    return [(a * NX + x, b * NX + x) for a, b in pairs for x in range(PANELS)]


def gather_row(block, y_index, core_index):
    stack = [block] + [lax.ppermute(block, "row", row_perm(s)) for s in (1, 2, 3)]
    mine = jnp.take(jnp.stack(stack), (y_index - jnp.arange(NY)) % NY, axis=0)
    swap = [(2 * y + core, 2 * y + 1 - core) for y in range(NY) for core in range(2)]
    other = lax.ppermute(mine, "row", swap)
    first = jnp.where(core_index == 0, mine, other)
    second = jnp.where(core_index == 0, other, mine)
    return jnp.stack([first, second], axis=1).reshape((2 * NY,) + block.shape)


def shards(cov):
    row = lax.axis_index("row")
    col = lax.axis_index("col")
    y_index, core_index = row // 2, row % 2
    z_index, x_index = col // NX, col % NX
    top = cov[0].reshape(NB, 2 * NB)
    piece = lax.all_to_all(top, "row", 0, 0, tiled=True)[: K // 8]

    turn = [
        (rr * 32 + g * 8 + m, m * 32 + g * 8 + rr)
        for rr in range(8)
        for g in range(4)
        for m in range(8)
    ]
    turned = lax.ppermute(piece, ("row", "col"), turn)
    rows_t = lax.all_gather(turned, "col", axis=0).reshape(4, K, 2 * NB)

    part = piece[:, :NB]
    for step in (4, 2, 1):
        got = lax.ppermute(part, "col", z_perm(step))
        part = jnp.where(z_index % (2 * step) == step, got, part)
    around = [part] + [lax.ppermute(part, "col", x_perm(s, PANELS)) for s in (1, 2, 3)]
    wide = jnp.take(jnp.stack(around), (x_index - jnp.arange(PANELS)) % NX, axis=0)
    wide = wide.transpose(1, 0, 2).reshape(K // 8, K)
    diag = gather_row(wide, y_index, core_index)
    diag = diag.reshape(8, PANELS, 32, K).transpose(1, 0, 2, 3).reshape(K, K)

    mine = gather_row(piece, y_index, core_index).reshape(K, 2 * NB)

    low = jnp.linalg.cholesky(diag, symmetrize_input=False)
    inv = lax.linalg.triangular_solve(low, jnp.eye(K, dtype=jnp.float32), left_side=True, lower=True)
    inv_p = inv.reshape(K, PANELS, 8, 32).transpose(0, 2, 1, 3).reshape(K, K)
    half = jnp.dot(inv_p, mine, precision=HI)
    weights = lax.dot_general(inv_p, half, (((0,), (0,)), ((), ())), precision=HI)
    panel = jnp.minimum(col, PANELS - 1)
    solve = lax.dynamic_slice(inv_p, (panel * NB, 0), (NB, K)).T
    in_panel = col < PANELS
    left = jnp.where(in_panel, -solve, weights[:, :NB])
    weights = jnp.concatenate([left, weights[:, NB:]], axis=1)

    product = lax.dot_general(rows_t, weights, (((1,), (0,)), ((), ())), precision=HI)
    product = product.reshape(4, 2, NB, 2, NB).transpose(1, 0, 2, 3, 4).reshape(8, NB, 2, NB)
    drop = in_panel & (jnp.arange(2) == 0)
    out = jnp.where(drop[None, None, :, None], 0.0, cov) - product
    tile = lax.dynamic_slice(low, (jnp.minimum(row, PANELS - 1) * NB, panel * NB), (NB, NB))
    tile = jnp.where(in_panel, tile, 0.0)
    first = jnp.stack([tile, jnp.zeros_like(tile)], axis=1)
    is_top = (jnp.arange(8) == 0) & (row < PANELS)
    return jnp.where(is_top[:, None, None, None], first[None], out)


def solution(mesh):
    return jax.shard_map(
        shards,
        mesh=mesh,
        in_specs=(P(None, "row", None, "col"),),
        out_specs=P(None, "row", None, "col"),
        check_vma=False,
    )
```

```python
import jax
import jax.numpy as jnp
from jax import lax
from jax.experimental import pallas as pl
from jax.experimental.pallas import tpu as pltpu
from jax.sharding import PartitionSpec as P

NB = 256
PANELS = 3
K = PANELS * NB
NY, NX, NZ = 4, 4, 8
HI = lax.Precision.HIGHEST
F32 = jnp.float32
BASE = 128
GROUP = 8


def dot(a, b, over):
    return lax.dot_general(a, b, (over, ((), ())), precision=HI, preferred_element_type=F32)


def factor_base(block):
    count = BASE // GROUP
    sub = lax.broadcasted_iota(jnp.int32, (GROUP, BASE), 0)
    lane = lax.broadcasted_iota(jnp.int32, (GROUP, BASE), 1)
    rows = [block[GROUP * h : GROUP * h + GROUP, :] for h in range(count)]
    unit = [jnp.where(lane == sub + GROUP * h, 1.0, 0.0).astype(F32) for h in range(count)]

    def spread_row(a, i):
        return jnp.broadcast_to(a[i : i + 1, :], (GROUP, BASE))

    def spread_lane(a, j):
        return jnp.broadcast_to(a[:, j : j + 1], (GROUP, BASE))

    upper, inverse = [], []
    for g in range(count):
        vs, vi = rows[g], unit[g]
        pivot = [spread_lane(vs, GROUP * g + j) for j in range(GROUP)]
        us = jnp.zeros((GROUP, BASE), F32)
        ui = us
        for i in range(GROUP):
            d = spread_row(pivot[i], i)
            recip = 1.0 / d
            root = lax.rsqrt(d)
            here = sub == i
            scale = pivot[i] * recip
            bs, bi = spread_row(vs, i), spread_row(vi, i)
            us = jnp.where(here, bs * root, us)
            ui = jnp.where(here, bi * root, ui)
            for j in range(i + 1, GROUP):
                b = spread_row(pivot[j], i)
                pivot[j] = jnp.where(here, b * recip, pivot[j] - scale * b)
            vs = jnp.where(here, bs * recip, vs - scale * bs)
            vi = jnp.where(here, bi * recip, vi - scale * bi)
        upper.append(us)
        inverse.append(ui)
        zs = [spread_row(vs, k) for k in range(GROUP)]
        zi = [spread_row(vi, k) for k in range(GROUP)]
        for h in range(g + 1, count):
            a, b = rows[h], unit[h]
            for k in range(GROUP):
                c = spread_lane(rows[h], GROUP * g + k)
                a = a - c * zs[k]
                b = b - c * zi[k]
            rows[h], unit[h] = a, b
    return jnp.concatenate(upper, 0), jnp.concatenate(inverse, 0)


def factor_kernel(d_ref, lt_ref, inv_ref):
    lt_ref[...] = d_ref[...]
    inv_ref[...] = jnp.zeros((K, K), F32)
    count = K // BASE
    for j in range(count):
        o, e = j * BASE, (j + 1) * BASE
        xs, xi = factor_base(lt_ref[o:e, o:e])
        lt_ref[o:e, o:e] = xs
        if j:
            inv_ref[o:e, :o] = dot(xi, inv_ref[o:e, :o], ((1,), (0,)))
        inv_ref[o:e, o:e] = xi
        if j < count - 1:
            p = dot(xi, lt_ref[o:e, e:], ((1,), (0,)))
            lt_ref[o:e, e:] = p
            lt_ref[e:, e:] = lt_ref[e:, e:] - dot(p, p, ((0,), (0,)))
            inv_ref[e:, :e] = inv_ref[e:, :e] - dot(p, inv_ref[o:e, :e], ((0,), (0,)))


def factor(diag):
    return pl.pallas_call(
        factor_kernel,
        out_shape=[jax.ShapeDtypeStruct((K, K), F32)] * 2,
        compiler_params=pltpu.CompilerParams(vmem_limit_bytes=40 * 2**20),
        cost_estimate=pl.CostEstimate(flops=4 * 10**9, bytes_accessed=10**7, transcendentals=0),
    )(diag)


def update_kernel(flag_ref, rows_ref, weights_ref, tile_ref, cov_ref, out_ref):
    product = dot(rows_ref[0], weights_ref[...], ((0,), (0,)))
    keep = 1.0 - flag_ref[0, 1].astype(F32)
    for l in range(2):
        for half in range(2):
            place = pl.ds(2 * half + l, NB, stride=4)
            base = cov_ref[0, place, :]
            if l == 0:
                base = jnp.where(keep > 0.0, base, 0.0)
            at = l * NB + half * 128
            out_ref[0, place, :] = base - product[:, at : at + 128]

    @pl.when((pl.program_id(0) == 0) & (flag_ref[0, 0] == 1))
    def _():
        for half in range(2):
            out_ref[0, pl.ds(2 * half, NB, stride=4), :] = tile_ref[:, half * 128 : half * 128 + 128]
            out_ref[0, pl.ds(2 * half + 1, NB, stride=4), :] = jnp.zeros((NB, 128), F32)


def update(flags, rows_t, weights, tile, cov):
    return pl.pallas_call(
        update_kernel,
        grid=(8,),
        in_specs=[
            pl.BlockSpec(memory_space=pltpu.SMEM),
            pl.BlockSpec((1, K, NB), lambda k: (k % 4, 0, k // 4)),
            pl.BlockSpec((K, 2 * NB), lambda k: (0, 0)),
            pl.BlockSpec((NB, NB), lambda k: (0, 0)),
            pl.BlockSpec((1, 4 * NB, 128), lambda k: (k, 0, 0)),
        ],
        out_specs=pl.BlockSpec((1, 4 * NB, 128), lambda k: (k, 0, 0)),
        out_shape=jax.ShapeDtypeStruct((8, 4 * NB, 128), F32),
        compiler_params=pltpu.CompilerParams(vmem_limit_bytes=40 * 2**20),
        cost_estimate=pl.CostEstimate(flops=10**10, bytes_accessed=16 * 10**6, transcendentals=0),
    )(flags, rows_t, weights, tile, cov)


def row_perm(shift):
    return [(y * 2 + core, ((y + shift) % NY) * 2 + core) for y in range(NY) for core in range(2)]


def x_perm(shift, limit):
    return [(z * NX + x, z * NX + (x + shift) % NX) for z in range(NZ) for x in range(limit)]


def z_perm(step):
    pairs = [(z, z + step) for z in range(0, NZ, 2 * step)]
    return [(a * NX + x, b * NX + x) for a, b in pairs for x in range(PANELS)]


def gather_row(block, y_index, core_index):
    stack = [block] + [lax.ppermute(block, "row", row_perm(s)) for s in (1, 2, 3)]
    mine = jnp.take(jnp.stack(stack), (y_index - jnp.arange(NY)) % NY, axis=0)
    swap = [(2 * y + core, 2 * y + 1 - core) for y in range(NY) for core in range(2)]
    other = lax.ppermute(mine, "row", swap)
    first = jnp.where(core_index == 0, mine, other)
    second = jnp.where(core_index == 0, other, mine)
    both = jnp.stack([first, second], axis=1).reshape(8, PANELS, 32, block.shape[1])
    return both.transpose(1, 0, 2, 3).reshape(K, block.shape[1])


def shards(covariance):
    row = lax.axis_index("row")
    col = lax.axis_index("col")
    y_index, core_index = row // 2, row % 2
    z_index, x_index = col // NX, col % NX
    top = covariance[0].reshape(NB, 2 * NB)
    cov = covariance.reshape(8, NB, 2, 2, 128).transpose(0, 1, 3, 2, 4).reshape(8, 4 * NB, 128)
    piece = lax.all_to_all(top, "row", 0, 0, tiled=True)[: K // 8]

    turn = [
        (rr * 32 + g * 8 + m, m * 32 + g * 8 + rr)
        for rr in range(8)
        for g in range(4)
        for m in range(8)
    ]
    turned = lax.ppermute(piece, ("row", "col"), turn)
    rows_t = lax.all_gather(turned, "col", axis=0).reshape(4, K, 2 * NB)

    part = piece[:, :NB]
    for step in (4, 2, 1):
        got = lax.ppermute(part, "col", z_perm(step))
        part = jnp.where(z_index % (2 * step) == step, got, part)
    around = [part] + [lax.ppermute(part, "col", x_perm(s, PANELS)) for s in (1, 2, 3)]
    wide = jnp.take(jnp.stack(around), (x_index - jnp.arange(PANELS)) % NX, axis=0)
    wide = wide.transpose(1, 0, 2).reshape(K // 8, K)
    diag = gather_row(wide, y_index, core_index)
    mine = gather_row(piece, y_index, core_index)

    upper, inverse = factor(diag)
    half = dot(inverse, mine, ((1,), (0,)))
    weights = dot(inverse, half, ((0,), (0,)))
    p_row = jnp.minimum(row, PANELS - 1)
    p_col = jnp.minimum(col, PANELS - 1)
    in_panel = col < PANELS
    solve = lax.dynamic_slice(inverse, (p_col * NB, 0), (NB, K)).T
    left = jnp.where(in_panel, -solve, weights[:, :NB])
    weights = jnp.concatenate([left, weights[:, NB:]], axis=1)
    weights = weights.reshape(PANELS, 8, 32, 2 * NB).transpose(1, 0, 2, 3).reshape(K, 2 * NB)

    tile = lax.dynamic_slice(upper, (p_col * NB, p_row * NB), (NB, NB))
    tile = jnp.where(p_row == p_col, jnp.triu(tile), tile).T
    tile = jnp.where(in_panel & (p_row >= p_col), tile, 0.0)
    flags = jnp.stack([row < PANELS, in_panel]).astype(jnp.int32).reshape(1, 2)
    out = update(flags, rows_t, weights, tile, cov)
    return out.reshape(8, NB, 2, 2, 128).transpose(0, 1, 3, 2, 4).reshape(8, NB, 2, NB)


def solution(mesh):
    return jax.shard_map(
        shards,
        mesh=mesh,
        in_specs=(P(None, "row", None, "col"),),
        out_specs=P(None, "row", None, "col"),
        check_vma=False,
    )
```

```python
import jax
import jax.numpy as jnp
from jax import lax
from jax.experimental import pallas as pl
from jax.experimental.pallas import tpu as pltpu
from jax.sharding import PartitionSpec as P

NB = 256
PANELS = 3
K = PANELS * NB
NY, NX, NZ = 4, 4, 8
HI = lax.Precision.HIGHEST
F32 = jnp.float32
BASE = 128
GROUP = 8


def dot(a, b, over):
    return lax.dot_general(a, b, (over, ((), ())), precision=HI, preferred_element_type=F32)


def factor_base(block):
    count = BASE // GROUP
    sub = lax.broadcasted_iota(jnp.int32, (GROUP, BASE), 0)
    lane = lax.broadcasted_iota(jnp.int32, (GROUP, BASE), 1)
    rows = [block[GROUP * h : GROUP * h + GROUP, :] for h in range(count)]
    unit = [jnp.where(lane == sub + GROUP * h, 1.0, 0.0).astype(F32) for h in range(count)]

    def spread_row(a, i):
        return jnp.broadcast_to(a[i : i + 1, :], (GROUP, BASE))

    def spread_lane(a, j):
        return jnp.broadcast_to(a[:, j : j + 1], (GROUP, BASE))

    upper, inverse = [], []
    for g in range(count):
        vs, vi = rows[g], unit[g]
        pivot = [spread_lane(vs, GROUP * g + j) for j in range(GROUP)]
        us = jnp.zeros((GROUP, BASE), F32)
        ui = us
        for i in range(GROUP):
            d = spread_row(pivot[i], i)
            recip = 1.0 / d
            root = lax.rsqrt(d)
            here = sub == i
            scale = pivot[i] * recip
            bs, bi = spread_row(vs, i), spread_row(vi, i)
            us = jnp.where(here, bs * root, us)
            ui = jnp.where(here, bi * root, ui)
            for j in range(i + 1, GROUP):
                b = spread_row(pivot[j], i)
                pivot[j] = jnp.where(here, b * recip, pivot[j] - scale * b)
            vs = jnp.where(here, bs * recip, vs - scale * bs)
            vi = jnp.where(here, bi * recip, vi - scale * bi)
        upper.append(us)
        inverse.append(ui)
        zs = [spread_row(vs, k) for k in range(GROUP)]
        zi = [spread_row(vi, k) for k in range(GROUP)]
        for h in range(g + 1, count):
            a, b = rows[h], unit[h]
            for k in range(GROUP):
                c = spread_lane(rows[h], GROUP * g + k)
                a = a - c * zs[k]
                b = b - c * zi[k]
            rows[h], unit[h] = a, b
    return jnp.concatenate(upper, 0), jnp.concatenate(inverse, 0)


def factor_kernel(at_ref, da_ref, db_ref, ua_ref, ub_ref, hi_ref, lo_ref, tile_ref, lt_ref, inv_ref, u_ref):
    row, col = at_ref[0], at_ref[1]
    y_index, core = row // 2, row % 2
    for s in range(NY):
        y_from = (y_index + NY - s) % NY
        for d_from, u_from, which in ((da_ref, ua_ref, core), (db_ref, ub_ref, 1 - core)):
            at = 32 * (2 * y_from + which)
            for p in range(PANELS):
                place = pl.ds(pl.multiple_of(p * NB + at, 32), 32)
                lt_ref[place, :] = d_from[s, p * 32 : p * 32 + 32, :]
                u_ref[place, :] = u_from[s, p * 32 : p * 32 + 32, :]
    inv_ref[...] = jnp.zeros((K, K), F32)
    count = K // BASE
    for j in range(count):
        o, e = j * BASE, (j + 1) * BASE
        xs, xi = factor_base(lt_ref[o:e, o:e])
        lt_ref[o:e, o:e] = xs
        if j:
            inv_ref[o:e, :o] = dot(xi, inv_ref[o:e, :o], ((1,), (0,)))
        inv_ref[o:e, o:e] = xi
        if j < count - 1:
            p = dot(xi, lt_ref[o:e, e:], ((1,), (0,)))
            lt_ref[o:e, e:] = p
            lt_ref[e:, e:] = lt_ref[e:, e:] - dot(p, p, ((0,), (0,)))
            inv_ref[e:, :e] = inv_ref[e:, :e] - dot(p, inv_ref[o:e, :e], ((0,), (0,)))

    for j in range(PANELS - 1, -1, -1):
        o, e = j * NB, (j + 1) * NB
        u_ref[o:e, :] = dot(inv_ref[o:e, :e], u_ref[:e, :], ((1,), (0,)))

    @pl.when(col < PANELS)
    def _():
        sub = lax.broadcasted_iota(jnp.int32, (K, NB), 0)
        lane = lax.broadcasted_iota(jnp.int32, (K, NB), 1)
        u_ref[:, :NB] = jnp.where(sub == lane + col * NB, -1.0, 0.0).astype(F32)

    for j in range(PANELS):
        o, e = j * NB, (j + 1) * NB
        w = dot(inv_ref[o:, o:e], u_ref[o:, :], ((0,), (0,)))
        hi = w.astype(jnp.bfloat16)
        lo = (w - hi.astype(F32)).astype(jnp.bfloat16)
        for r in range(8):
            to, frm = r * 96 + j * 32, r * 32
            hi_ref[to : to + 32, :] = hi[frm : frm + 32, :]
            lo_ref[to : to + 32, :] = lo[frm : frm + 32, :]

    tile_ref[...] = jnp.zeros((NB, NB), F32)

    @pl.when((col < PANELS) & (row < PANELS) & (row >= col))
    def _():
        p_row = pl.multiple_of(row * NB, NB)
        p_col = pl.multiple_of(col * NB, NB)
        part = lt_ref[pl.ds(p_col, NB), pl.ds(p_row, NB)]
        sub = lax.broadcasted_iota(jnp.int32, (NB, NB), 0)
        lane = lax.broadcasted_iota(jnp.int32, (NB, NB), 1)
        tile_ref[...] = jnp.where((row > col) | (lane >= sub), part, 0.0).T


def factor(place, da, db, ua, ub):
    vmem = pl.BlockSpec(memory_space=pltpu.VMEM)
    return pl.pallas_call(
        factor_kernel,
        in_specs=[pl.BlockSpec(memory_space=pltpu.SMEM)] + [vmem] * 4,
        out_specs=[vmem] * 3,
        out_shape=[
            jax.ShapeDtypeStruct((K, 2 * NB), jnp.bfloat16),
            jax.ShapeDtypeStruct((K, 2 * NB), jnp.bfloat16),
            jax.ShapeDtypeStruct((NB, NB), F32),
        ],
        scratch_shapes=[
            pltpu.VMEM((K, K), F32),
            pltpu.VMEM((K, K), F32),
            pltpu.VMEM((K, 2 * NB), F32),
        ],
        compiler_params=pltpu.CompilerParams(vmem_limit_bytes=40 * 2**20),
        cost_estimate=pl.CostEstimate(flops=4 * 10**9, bytes_accessed=10**7, transcendentals=0),
    )(place, da, db, ua, ub)


def update_kernel(at_ref, rows_ref, hi_ref, lo_ref, tile_ref, cov_ref, out_ref):
    over = (((0,), (0,)), ((), ()))
    rows = rows_ref[0]
    hi = rows.astype(jnp.bfloat16)
    lo = (rows - hi.astype(F32)).astype(jnp.bfloat16)
    product = lax.dot_general(hi, hi_ref[...], over, preferred_element_type=F32)
    product += lax.dot_general(hi, lo_ref[...], over, preferred_element_type=F32)
    product += lax.dot_general(lo, hi_ref[...], over, preferred_element_type=F32)
    in_panel = at_ref[1] < PANELS
    for l in range(2):
        for half in range(2):
            place = pl.ds(2 * half + l, NB, stride=4)
            base = cov_ref[0, place, :]
            if l == 0:
                base = jnp.where(in_panel, 0.0, base)
            at = l * NB + half * 128
            out_ref[0, place, :] = base - product[:, at : at + 128]

    @pl.when((pl.program_id(0) == 0) & (at_ref[0] < PANELS))
    def _():
        for half in range(2):
            out_ref[0, pl.ds(2 * half, NB, stride=4), :] = tile_ref[:, half * 128 : half * 128 + 128]
            out_ref[0, pl.ds(2 * half + 1, NB, stride=4), :] = jnp.zeros((NB, 128), F32)


def update(place, rows_t, hi, lo, tile, cov):
    return pl.pallas_call(
        update_kernel,
        grid=(8,),
        in_specs=[
            pl.BlockSpec(memory_space=pltpu.SMEM),
            pl.BlockSpec((1, K, NB), lambda k: (k % 4, 0, k // 4)),
            pl.BlockSpec((K, 2 * NB), lambda k: (0, 0)),
            pl.BlockSpec((K, 2 * NB), lambda k: (0, 0)),
            pl.BlockSpec((NB, NB), lambda k: (0, 0)),
            pl.BlockSpec((1, 4 * NB, 128), lambda k: (k, 0, 0)),
        ],
        out_specs=pl.BlockSpec((1, 4 * NB, 128), lambda k: (k, 0, 0)),
        out_shape=jax.ShapeDtypeStruct((8, 4 * NB, 128), F32),
        compiler_params=pltpu.CompilerParams(vmem_limit_bytes=40 * 2**20),
        cost_estimate=pl.CostEstimate(flops=5 * 10**9, bytes_accessed=16 * 10**6, transcendentals=0),
    )(place, rows_t, hi, lo, tile, cov)


def row_perm(shift):
    return [(y * 2 + core, ((y + shift) % NY) * 2 + core) for y in range(NY) for core in range(2)]


def x_perm(shift, limit):
    return [(z * NX + x, z * NX + (x + shift) % NX) for z in range(NZ) for x in range(limit)]


def z_perm(step):
    pairs = [(z, z + step) for z in range(0, NZ, 2 * step)]
    return [(a * NX + x, b * NX + x) for a, b in pairs for x in range(PANELS)]


CORES = [(2 * y + core, 2 * y + 1 - core) for y in range(NY) for core in range(2)]


def gather_row(block):
    mine = jnp.stack([block] + [lax.ppermute(block, "row", row_perm(s)) for s in (1, 2, 3)])
    return mine, lax.ppermute(mine, "row", CORES)


def shards(covariance):
    row = lax.axis_index("row")
    col = lax.axis_index("col")
    place = jnp.stack([row, col]).astype(jnp.int32)
    z_index, x_index = col // NX, col % NX
    top = covariance[0].reshape(NB, 2 * NB)
    cov = covariance.reshape(8, NB, 2, 2, 128).transpose(0, 1, 3, 2, 4).reshape(8, 4 * NB, 128)
    piece = lax.all_to_all(top, "row", 0, 0, tiled=True)[: K // 8]

    part = piece[:, :NB]
    for step in (4, 2, 1):
        got = lax.ppermute(part, "col", z_perm(step))
        part = jnp.where(z_index % (2 * step) == step, got, part)
        if step == 4:
            piece_turn, part = lax.optimization_barrier((piece, part))
    around = [part] + [lax.ppermute(part, "col", x_perm(s, PANELS)) for s in (1, 2, 3)]
    wide = []
    for q in range(PANELS):
        s = (x_index + NX - q) % NX
        pick = jnp.where(s < 2, jnp.where(s == 0, around[0], around[1]), jnp.where(s == 2, around[2], around[3]))
        wide.append(pick)
    da, db = gather_row(jnp.concatenate(wide, axis=1))
    ua, ub = gather_row(piece)

    turn = [
        (rr * 32 + g * 8 + m, m * 32 + g * 8 + rr)
        for rr in range(8)
        for g in range(4)
        for m in range(8)
    ]
    turned = lax.ppermute(piece_turn, ("row", "col"), turn)
    rows_t = lax.all_gather(turned, "col", axis=0).reshape(4, K, 2 * NB)

    hi, lo, tile = factor(place, da, db, ua, ub)
    out = update(place, rows_t, hi, lo, tile, cov)
    return out.reshape(8, NB, 2, 2, 128).transpose(0, 1, 3, 2, 4).reshape(8, NB, 2, NB)


def solution(mesh):
    return jax.shard_map(
        shards,
        mesh=mesh,
        in_specs=(P(None, "row", None, "col"),),
        out_specs=P(None, "row", None, "col"),
        check_vma=False,
    )
```

```python
import functools

import jax
import jax.numpy as jnp
from jax import lax
from jax.experimental import pallas as pl
from jax.experimental.pallas import tpu as pltpu
from jax.sharding import PartitionSpec as P

NB = 256
PANELS = 3
K = PANELS * NB
NY, NX, NZ = 4, 4, 8
HI = lax.Precision.HIGHEST
F32 = jnp.float32
BASE = 128
GROUP = 8


def dot(a, b, over):
    return lax.dot_general(a, b, (over, ((), ())), precision=HI, preferred_element_type=F32)


ROWS = ((1,), (0,))
TURN = ((0,), (0,))


def total(terms):
    while len(terms) > 1:
        terms = [terms[i] + terms[i + 1] if i + 1 < len(terms) else terms[i] for i in range(0, len(terms), 2)]
    return terms[0]


def factor_base(block, tasks):
    count = BASE // GROUP
    sub = lax.broadcasted_iota(jnp.int32, (GROUP, BASE), 0)
    lane = lax.broadcasted_iota(jnp.int32, (GROUP, BASE), 1)
    rows = [block[GROUP * h : GROUP * h + GROUP, :] for h in range(count)]

    def spread_row(a, i):
        return jnp.broadcast_to(a[i : i + 1, :], (GROUP, BASE))

    def spread_lane(a, j):
        return jnp.broadcast_to(a[:, j : j + 1], (GROUP, BASE))

    upper, inverse = [], []
    each = -(-len(tasks) // (count - 1))
    for g in range(count):
        lo, hi = GROUP * g, GROUP * g + GROUP
        inside = (lane >= lo) & (lane < hi)
        old = rows[g]
        pivot = [spread_lane(old, lo + j) for j in range(GROUP)]
        v = jnp.where(inside, jnp.where(lane == sub + lo, 1.0, 0.0), old)
        x = jnp.zeros((GROUP, BASE), F32)
        diag = jnp.ones((GROUP, BASE), F32)
        for i in range(GROUP):
            here = sub == i
            d = spread_row(pivot[i], i)
            scale = jnp.where(here, 0.0, pivot[i]) / d
            b = spread_row(v, i)
            x = jnp.where(here, b, x)
            diag = jnp.where(here, d, diag)
            for j in range(i + 1, GROUP):
                pivot[j] = pivot[j] - scale * spread_row(pivot[j], i)
            v = v - scale * b
        z = v / diag
        zs = [spread_row(z, k) for k in range(GROUP)]
        for h in range(g + 1, count):
            terms = [spread_lane(rows[h], lo + k) * zs[k] for k in range(GROUP)]
            rows[h] = jnp.where(inside, 0.0, rows[h]) - total(terms)
        x = x * lax.rsqrt(diag)
        corner = total([spread_lane(x, lo + k) * spread_row(old, k) for k in range(GROUP)])
        upper.append(jnp.where(lane >= hi, x, jnp.where(lane >= lo, corner, 0.0)))
        inverse.append(jnp.where(lane < hi, x, 0.0))
        for _ in range(each):
            if tasks:
                tasks.pop(0)()
    while tasks:
        tasks.pop(0)()
    return jnp.concatenate(upper, 0), jnp.concatenate(inverse, 0)


def factor_all(lt, inv, u, w, col):
    inv[...] = jnp.zeros((K, K), F32)
    w[...] = jnp.zeros((K, 2 * NB), F32)
    in_panel = col < PANELS
    block = lt[:BASE, :BASE]
    tasks = []
    for o in range(0, K, BASE):
        e = o + BASE
        xs, xi = factor_base(block, tasks)
        lt[o:e, o:e] = xs
        inv[o:e, o:e] = xi
        if e < K:
            n = e + BASE
            near = dot(xi, lt[o:e, e:n], ROWS)
            block = lt[e:n, e:n] - dot(near, near, TURN)
            lt[o:e, e:n] = near

        def panel(o=o, e=e, xi=xi):
            if e + BASE < K:
                lt[o:e, e + BASE :] = dot(xi, lt[o:e, e + BASE :], ROWS)

        def solve(o=o, e=e, xi=xi):
            u[o:e, :] = dot(xi, u[o:e, :], ROWS)

        def invert(o=o, e=e, xi=xi):
            if o:
                inv[o:e, :o] = dot(xi, inv[o:e, :o], ROWS)

        def weigh(o=o, e=e):
            sub = lax.broadcasted_iota(jnp.int32, (BASE, NB), 0)
            lane = lax.broadcasted_iota(jnp.int32, (BASE, NB), 1)
            unit = jnp.where(sub + o == lane + col * NB, -1.0, 0.0).astype(F32)
            left = jnp.where(in_panel, unit, u[o:e, :NB])
            right = u[o:e, NB:]
            for c in range(0, e, NB):
                t = min(c + NB, e)
                w[c:t, :NB] = w[c:t, :NB] + dot(inv[o:e, c:t], left, TURN)
                w[c:t, NB:] = w[c:t, NB:] + dot(inv[o:e, c:t], right, TURN)

        def trail(b, o=o, e=e):
            t = b + BASE
            p = lt[o:e, b:t]
            if b > e:
                lt[b:t, b:] = lt[b:t, b:] - dot(p, lt[o:e, b:], TURN)
            elif t < K:
                lt[b:t, t:] = lt[b:t, t:] - dot(p, lt[o:e, t:], TURN)

        def trail_inv(b, o=o, e=e):
            inv[b : b + BASE, :e] = inv[b : b + BASE, :e] - dot(lt[o:e, b : b + BASE], inv[o:e, :e], TURN)

        def trail_u(b, o=o, e=e):
            u[b : b + BASE, :] = u[b : b + BASE, :] - dot(lt[o:e, b : b + BASE], u[o:e, :], TURN)

        later = range(e, K, BASE)
        tasks = [panel] + [functools.partial(trail, b) for b in later] + [invert, solve]
        tasks += [functools.partial(trail_inv, b) for b in later]
        tasks += [functools.partial(trail_u, b) for b in later] + [weigh]
    while tasks:
        tasks.pop(0)()


def factor_kernel(at_ref, da_ref, db_ref, weights_ref, tile_ref, lt, inv, u, w, split, tile, sem):
    row, col = at_ref[0], at_ref[1]
    y_index, core = row // 2, row % 2
    for s in range(NY):
        y_from = (y_index + NY - s) % NY
        for d_from, which in ((da_ref, core), (db_ref, 1 - core)):
            at = 32 * (2 * y_from + which)
            lane = 0
            for p in range(PANELS):
                place = pl.ds(pl.multiple_of(p * NB + at, 32), 32)
                wide = K - p * NB
                lt[place, p * NB :] = d_from[s, :, lane : lane + wide]
                lane += wide
            for p in range(PANELS):
                place = pl.ds(pl.multiple_of(p * NB + at, 32), 32)
                u[place, :] = d_from[s, :, lane : lane + 2 * NB]
                lane += 2 * NB
    factor_all(lt, inv, u, w, col)

    for j in range(PANELS):
        o, e = j * NB, (j + 1) * NB
        hi = w[o:e, :].astype(jnp.bfloat16)
        lo = (w[o:e, :] - hi.astype(F32)).astype(jnp.bfloat16)
        for r in range(8):
            to, frm = r * 96 + j * 32, r * 32
            split[to : to + 32, : 2 * NB] = hi[frm : frm + 32, :]
            split[to : to + 32, 2 * NB :] = lo[frm : frm + 32, :]
    send = pltpu.make_async_copy(split, weights_ref, sem.at[0])
    send.start()

    tile[...] = jnp.zeros((NB, NB), F32)

    @pl.when((col < PANELS) & (row < PANELS) & (row >= col))
    def _():
        p_row = pl.multiple_of(row * NB, NB)
        p_col = pl.multiple_of(col * NB, NB)
        part = lt[pl.ds(p_col, NB), pl.ds(p_row, NB)]
        sub = lax.broadcasted_iota(jnp.int32, (NB, NB), 0)
        lane = lax.broadcasted_iota(jnp.int32, (NB, NB), 1)
        tile[...] = jnp.where((row > col) | (lane >= sub), part, 0.0).T

    send_tile = pltpu.make_async_copy(tile, tile_ref, sem.at[1])
    send_tile.start()
    send.wait()
    send_tile.wait()


def factor(place, da, db):
    vmem = pl.BlockSpec(memory_space=pltpu.VMEM)
    hbm = pl.BlockSpec(memory_space=pltpu.HBM)
    return pl.pallas_call(
        factor_kernel,
        in_specs=[pl.BlockSpec(memory_space=pltpu.SMEM), vmem, vmem],
        out_specs=[hbm, hbm],
        out_shape=[
            jax.ShapeDtypeStruct((K, 4 * NB), jnp.bfloat16),
            jax.ShapeDtypeStruct((NB, NB), F32),
        ],
        scratch_shapes=[
            pltpu.VMEM((K, K), F32),
            pltpu.VMEM((K, K), F32),
            pltpu.VMEM((K, 2 * NB), F32),
            pltpu.VMEM((K, 2 * NB), F32),
            pltpu.VMEM((K, 4 * NB), jnp.bfloat16),
            pltpu.VMEM((NB, NB), F32),
            pltpu.SemaphoreType.DMA((2,)),
        ],
        compiler_params=pltpu.CompilerParams(vmem_limit_bytes=28 * 2**20),
        cost_estimate=pl.CostEstimate(flops=4 * 10**9, bytes_accessed=10**7, transcendentals=0),
        name="factor",
    )(place, da, db)


def update_kernel(
    at_ref, weights_ref, tile_ref, cov_ref, rows_ref, out_ref, split, tile, buf, acc, own_sem, in_sem, cov_sem, out_sem
):
    row, col = at_ref[0], at_ref[1]

    def load(g):
        return pltpu.make_async_copy(rows_ref.at[g], buf.at[g], in_sem.at[g])

    def base(k):
        return pltpu.make_async_copy(cov_ref.at[k], acc.at[k], cov_sem.at[k])

    def store(k):
        return pltpu.make_async_copy(acc.at[k], out_ref.at[k], out_sem.at[k])

    get_weights = pltpu.make_async_copy(weights_ref, split, own_sem.at[0])
    get_tile = pltpu.make_async_copy(tile_ref, tile, own_sem.at[1])
    load(0).start()
    get_weights.start()
    get_tile.start()
    for g in range(4):
        if g:
            load(g).start()
        base(g).start()
        base(g + 4).start()
    get_weights.wait()
    get_tile.wait()

    def step(g, carry):
        load(g).wait()
        base(g).wait()
        base(g + 4).wait()
        over = (TURN, ((), ()))
        for l in range(2):
            k = l * 4 + g
            rows = buf[g, :, l * NB : (l + 1) * NB]
            hi = rows.astype(jnp.bfloat16)
            lo = (rows - hi.astype(F32)).astype(jnp.bfloat16)
            both = lax.dot_general(hi, split[...], over, preferred_element_type=F32)
            small = lax.dot_general(lo, split[:, : 2 * NB], over, preferred_element_type=F32)
            product = both[:, : 2 * NB] + (both[:, 2 * NB :] + small)
            for q in range(4):
                place = pl.ds(q, NB, stride=4)
                at = (q % 2) * NB + (q // 2) * 128
                left = acc[k, place, :]
                if q % 2 == 0:
                    left = jnp.where(col < PANELS, 0.0, left)
                acc[k, place, :] = left - product[:, at : at + 128]

        @pl.when((g == 0) & (row < PANELS))
        def _():
            for part in range(2):
                acc[0, pl.ds(2 * part, NB, stride=4), :] = tile[:, part * 128 : part * 128 + 128]
                acc[0, pl.ds(2 * part + 1, NB, stride=4), :] = jnp.zeros((NB, 128), F32)

        store(g).start()
        store(g + 4).start()
        return carry

    lax.fori_loop(0, 4, step, 0)
    for k in range(8):
        store(k).wait()


def update(place, weights, tile, cov, rows_t):
    hbm = pl.BlockSpec(memory_space=pltpu.HBM)
    return pl.pallas_call(
        update_kernel,
        in_specs=[pl.BlockSpec(memory_space=pltpu.SMEM)] + [hbm] * 4,
        out_specs=hbm,
        out_shape=jax.ShapeDtypeStruct((8, 4 * NB, 128), F32),
        scratch_shapes=[
            pltpu.VMEM((K, 4 * NB), jnp.bfloat16),
            pltpu.VMEM((NB, NB), F32),
            pltpu.VMEM((4, K, 2 * NB), F32),
            pltpu.VMEM((8, 4 * NB, 128), F32),
            pltpu.SemaphoreType.DMA((2,)),
            pltpu.SemaphoreType.DMA((4,)),
            pltpu.SemaphoreType.DMA((8,)),
            pltpu.SemaphoreType.DMA((8,)),
        ],
        compiler_params=pltpu.CompilerParams(vmem_limit_bytes=60 * 2**20),
        cost_estimate=pl.CostEstimate(flops=5 * 10**9, bytes_accessed=16 * 10**6, transcendentals=0),
        name="update",
    )(place, weights, tile, cov, rows_t)


def row_perm(shift):
    return [(y * 2 + core, ((y + shift) % NY) * 2 + core) for y in range(NY) for core in range(2)]


def x_perm(shift, limit):
    return [(z * NX + x, z * NX + (x + shift) % NX) for z in range(NZ) for x in range(limit)]


def z_perm(step):
    pairs = [(z, z + step) for z in range(0, NZ, 2 * step)]
    return [(a * NX + x, b * NX + x) for a, b in pairs for x in range(PANELS)]


CORES = [(2 * y + core, 2 * y + 1 - core) for y in range(NY) for core in range(2)]


def after(arrays, *done):
    return lax.optimization_barrier((tuple(arrays), done))[0]


def gather_row(block):
    return [block] + [lax.ppermute(block, "row", row_perm(s)) for s in (1, 2, 3)]


def turn_pairs():
    return [(q * 32 + g * 8 + m, m * 32 + g * 8 + q) for q in range(8) for g in range(4) for m in range(8)]


def shards(covariance):
    row = lax.axis_index("row")
    col = lax.axis_index("col")
    place = jnp.stack([row, col]).astype(jnp.int32)
    z_index, x_index = col // NX, col % NX
    top = covariance[0].reshape(NB, 2 * NB)
    cov = covariance.reshape(8, NB, 2, 2, 128).transpose(0, 1, 3, 2, 4).reshape(8, 4 * NB, 128)
    piece = lax.all_to_all(top, "row", 0, 0, tiled=True)[: K // 8]

    turned = lax.ppermute(piece, ("row", "col"), turn_pairs())
    (part,) = after((piece[:, :NB],), place)
    for step in (4, 2, 1):
        got = lax.ppermute(part, "col", z_perm(step))
        part = jnp.where(z_index % (2 * step) == step, got, part)
        if step == 4:
            (turned,) = after((turned,), part)
    rows_t = lax.all_gather(turned, "col", axis=0).reshape(4, K, 2 * NB)

    around = [part] + [lax.ppermute(part, "col", x_perm(s, PANELS)) for s in (1, 2, 3)]
    wide = []
    for q in range(PANELS):
        s = (x_index + NX - q) % NX
        pick = jnp.where(s < 2, jnp.where(s == 0, around[0], around[1]), jnp.where(s == 2, around[2], around[3]))
        wide.append(pick)
    wide = [wide[q][32 * p : 32 * p + 32] for p in range(PANELS) for q in range(p, PANELS)]
    wide = jnp.concatenate(wide + [piece[32 * p : 32 * p + 32] for p in range(PANELS)], axis=1)
    da = jnp.stack(gather_row(wide))
    db = lax.ppermute(da, "row", CORES)

    weights, tile = factor(place, da, db)
    out = update(place, weights, tile, cov, rows_t)
    return out.reshape(8, NB, 2, 2, 128).transpose(0, 1, 3, 2, 4).reshape(8, NB, 2, NB)


def solution(mesh):
    return jax.shard_map(
        shards,
        mesh=mesh,
        in_specs=(P(None, "row", None, "col"),),
        out_specs=P(None, "row", None, "col"),
        check_vma=False,
    )
```

```python
import functools

import jax
import jax.numpy as jnp
from jax import lax
from jax.experimental import pallas as pl
from jax.experimental.pallas import tpu as pltpu
from jax.sharding import PartitionSpec as P

NB = 256
PANELS = 3
K = PANELS * NB
NY, NX, NZ = 4, 4, 8
HI = lax.Precision.HIGHEST
F32 = jnp.float32
BASE = 128
GROUP = 8


def dot(a, b, over):
    return lax.dot_general(a, b, (over, ((), ())), precision=HI, preferred_element_type=F32)


ROWS = ((1,), (0,))
TURN = ((0,), (0,))


def total(terms):
    while len(terms) > 1:
        terms = [terms[i] + terms[i + 1] if i + 1 < len(terms) else terms[i] for i in range(0, len(terms), 2)]
    return terms[0]


def factor_base(block, tasks):
    count = BASE // GROUP
    sub = lax.broadcasted_iota(jnp.int32, (GROUP, BASE), 0)
    lane = lax.broadcasted_iota(jnp.int32, (GROUP, BASE), 1)
    rows = [block[GROUP * h : GROUP * h + GROUP, :] for h in range(count)]

    def spread_row(a, i):
        return jnp.broadcast_to(a[i : i + 1, :], (GROUP, BASE))

    def spread_lane(a, j):
        return jnp.broadcast_to(a[:, j : j + 1], (GROUP, BASE))

    upper, inverse = [], []
    each = -(-len(tasks) // (count - 1))
    for g in range(count):
        lo, hi = GROUP * g, GROUP * g + GROUP
        inside = (lane >= lo) & (lane < hi)
        old = rows[g]
        pivot = [spread_lane(old, lo + j) for j in range(GROUP)]
        v = jnp.where(inside, jnp.where(lane == sub + lo, 1.0, 0.0), old)
        x = jnp.zeros((GROUP, BASE), F32)
        diag = jnp.ones((GROUP, BASE), F32)
        for i in range(GROUP):
            here = sub == i
            d = spread_row(pivot[i], i)
            scale = jnp.where(here, 0.0, pivot[i]) / d
            b = spread_row(v, i)
            x = jnp.where(here, b, x)
            diag = jnp.where(here, d, diag)
            for j in range(i + 1, GROUP):
                pivot[j] = pivot[j] - scale * spread_row(pivot[j], i)
            v = v - scale * b
        z = v / diag
        zs = [spread_row(z, k) for k in range(GROUP)]
        for h in range(g + 1, count):
            terms = [spread_lane(rows[h], lo + k) * zs[k] for k in range(GROUP)]
            rows[h] = jnp.where(inside, 0.0, rows[h]) - total(terms)
        x = x * lax.rsqrt(diag)
        corner = total([spread_lane(x, lo + k) * spread_row(old, k) for k in range(GROUP)])
        upper.append(jnp.where(lane >= hi, x, jnp.where(lane >= lo, corner, 0.0)))
        inverse.append(jnp.where(lane < hi, x, 0.0))
        for _ in range(each):
            if tasks:
                tasks.pop(0)()
    while tasks:
        tasks.pop(0)()
    return jnp.concatenate(upper, 0), jnp.concatenate(inverse, 0)


def factor_all(lt, inv, u, w, col):
    inv[...] = jnp.zeros((K, K), F32)
    w[...] = jnp.zeros((K, 2 * NB), F32)
    in_panel = col < PANELS
    block = lt[:BASE, :BASE]
    tasks = []
    for o in range(0, K, BASE):
        e = o + BASE
        xs, xi = factor_base(block, tasks)
        lt[o:e, o:e] = xs
        inv[o:e, o:e] = xi
        if e < K:
            n = e + BASE
            near = dot(xi, lt[o:e, e:n], ROWS)
            block = lt[e:n, e:n] - dot(near, near, TURN)
            lt[o:e, e:n] = near

        def panel(o=o, e=e, xi=xi):
            if e + BASE < K:
                lt[o:e, e + BASE :] = dot(xi, lt[o:e, e + BASE :], ROWS)

        def solve(o=o, e=e, xi=xi):
            u[o:e, :] = dot(xi, u[o:e, :], ROWS)

        def invert(o=o, e=e, xi=xi):
            if o:
                inv[o:e, :o] = dot(xi, inv[o:e, :o], ROWS)

        def weigh(o=o, e=e):
            sub = lax.broadcasted_iota(jnp.int32, (BASE, NB), 0)
            lane = lax.broadcasted_iota(jnp.int32, (BASE, NB), 1)
            unit = jnp.where(sub + o == lane + col * NB, -1.0, 0.0).astype(F32)
            left = jnp.where(in_panel, unit, u[o:e, :NB])
            right = u[o:e, NB:]
            for c in range(0, e, NB):
                t = min(c + NB, e)
                w[c:t, :NB] = w[c:t, :NB] + dot(inv[o:e, c:t], left, TURN)
                w[c:t, NB:] = w[c:t, NB:] + dot(inv[o:e, c:t], right, TURN)

        def trail(b, o=o, e=e):
            t = b + BASE
            p = lt[o:e, b:t]
            if b > e:
                lt[b:t, b:] = lt[b:t, b:] - dot(p, lt[o:e, b:], TURN)
            elif t < K:
                lt[b:t, t:] = lt[b:t, t:] - dot(p, lt[o:e, t:], TURN)

        def trail_inv(b, o=o, e=e):
            inv[b : b + BASE, :e] = inv[b : b + BASE, :e] - dot(lt[o:e, b : b + BASE], inv[o:e, :e], TURN)

        def trail_u(b, o=o, e=e):
            u[b : b + BASE, :] = u[b : b + BASE, :] - dot(lt[o:e, b : b + BASE], u[o:e, :], TURN)

        later = range(e, K, BASE)
        tasks = [panel] + [functools.partial(trail, b) for b in later] + [invert, solve]
        tasks += [functools.partial(trail_inv, b) for b in later]
        tasks += [functools.partial(trail_u, b) for b in later] + [weigh]
    while tasks:
        tasks.pop(0)()


def factor_kernel(at_ref, da_ref, db_ref, split, tile, lt, inv, u, w):
    row, col = at_ref[0], at_ref[1]
    y_index, core = row // 2, row % 2
    for s in range(NY):
        y_from = (y_index + NY - s) % NY
        for d_from, which in ((da_ref, core), (db_ref, 1 - core)):
            at = 32 * (2 * y_from + which)
            lane = 0
            for p in range(PANELS):
                place = pl.ds(pl.multiple_of(p * NB + at, 32), 32)
                wide = K - p * NB
                lt[place, p * NB :] = d_from[s, :, lane : lane + wide]
                lane += wide
            for p in range(PANELS):
                place = pl.ds(pl.multiple_of(p * NB + at, 32), 32)
                u[place, :] = d_from[s, :, lane : lane + 2 * NB]
                lane += 2 * NB
    factor_all(lt, inv, u, w, col)

    for j in range(PANELS):
        o, e = j * NB, (j + 1) * NB
        hi = w[o:e, :].astype(jnp.bfloat16)
        lo = (w[o:e, :] - hi.astype(F32)).astype(jnp.bfloat16)
        for r in range(8):
            to = pl.ds(pl.multiple_of((r ^ row) * 96 + j * 32, 32), 32)
            split[to, : 2 * NB] = hi[r * 32 : r * 32 + 32, :]
            split[to, 2 * NB :] = lo[r * 32 : r * 32 + 32, :]
    tile[...] = jnp.zeros((NB, NB), F32)

    @pl.when((col < PANELS) & (row < PANELS) & (row >= col))
    def _():
        p_row = pl.multiple_of(row * NB, NB)
        p_col = pl.multiple_of(col * NB, NB)
        part = lt[pl.ds(p_col, NB), pl.ds(p_row, NB)]
        sub = lax.broadcasted_iota(jnp.int32, (NB, NB), 0)
        lane = lax.broadcasted_iota(jnp.int32, (NB, NB), 1)
        tile[...] = jnp.where((row > col) | (lane >= sub), part, 0.0).T


def factor(place, da, db):
    vmem = pl.BlockSpec(memory_space=pltpu.VMEM)
    return pl.pallas_call(
        factor_kernel,
        in_specs=[pl.BlockSpec(memory_space=pltpu.SMEM), vmem, vmem],
        out_specs=[vmem] * 2,
        out_shape=[
            jax.ShapeDtypeStruct((K, 4 * NB), jnp.bfloat16),
            jax.ShapeDtypeStruct((NB, NB), F32),
        ],
        scratch_shapes=[
            pltpu.VMEM((K, K), F32),
            pltpu.VMEM((K, K), F32),
            pltpu.VMEM((K, 2 * NB), F32),
            pltpu.VMEM((K, 2 * NB), F32),
        ],
        compiler_params=pltpu.CompilerParams(vmem_limit_bytes=28 * 2**20),
        cost_estimate=pl.CostEstimate(flops=4 * 10**9, bytes_accessed=10**7, transcendentals=0),
        name="factor",
    )(place, da, db)


def update_kernel(at_ref, split, tile, cov_ref, rows_ref, out_ref, buf, acc, in_sem, cov_sem, out_sem):
    row, col = at_ref[0], at_ref[1]

    def load(g):
        return pltpu.make_async_copy(rows_ref.at[g], buf.at[g], in_sem.at[g])

    def base(k):
        return pltpu.make_async_copy(cov_ref.at[k], acc.at[k], cov_sem.at[k])

    def store(k):
        return pltpu.make_async_copy(acc.at[k], out_ref.at[k], out_sem.at[k])

    def fetch(g):
        load(g).start()
        base(g).start()
        base(g + 4).start()

    fetch(0)

    def step(g, carry):
        load(g).wait()
        base(g).wait()
        base(g + 4).wait()

        @pl.when(g < 3)
        def _():
            fetch(g + 1)

        over = (TURN, ((), ()))
        for l in range(2):
            k = l * 4 + g
            rows = buf[g, :, l * NB : (l + 1) * NB]
            hi = rows.astype(jnp.bfloat16)
            lo = (rows - hi.astype(F32)).astype(jnp.bfloat16)
            both = lax.dot_general(hi, split[...], over, preferred_element_type=F32)
            small = lax.dot_general(lo, split[:, : 2 * NB], over, preferred_element_type=F32)
            product = both[:, : 2 * NB] + (both[:, 2 * NB :] + small)
            for q in range(4):
                place = pl.ds(q, NB, stride=4)
                at = (q % 2) * NB + (q // 2) * 128
                left = acc[k, place, :]
                if q % 2 == 0:
                    left = jnp.where(col < PANELS, 0.0, left)
                acc[k, place, :] = left - product[:, at : at + 128]

        @pl.when((g == 0) & (row < PANELS))
        def _():
            for part in range(2):
                acc[0, pl.ds(2 * part, NB, stride=4), :] = tile[:, part * 128 : part * 128 + 128]
                acc[0, pl.ds(2 * part + 1, NB, stride=4), :] = jnp.zeros((NB, 128), F32)

        store(g).start()
        store(g + 4).start()
        return carry

    lax.fori_loop(0, 4, step, 0)
    for k in range(8):
        store(k).wait()


def update(place, weights, tile, cov, rows_t):
    vmem = pl.BlockSpec(memory_space=pltpu.VMEM)
    hbm = pl.BlockSpec(memory_space=pltpu.HBM)
    return pl.pallas_call(
        update_kernel,
        in_specs=[pl.BlockSpec(memory_space=pltpu.SMEM), vmem, vmem, hbm, hbm],
        out_specs=hbm,
        out_shape=jax.ShapeDtypeStruct((8, 4 * NB, 128), F32),
        scratch_shapes=[
            pltpu.VMEM((4, K, 2 * NB), F32),
            pltpu.VMEM((8, 4 * NB, 128), F32),
            pltpu.SemaphoreType.DMA((4,)),
            pltpu.SemaphoreType.DMA((8,)),
            pltpu.SemaphoreType.DMA((8,)),
        ],
        compiler_params=pltpu.CompilerParams(vmem_limit_bytes=50 * 2**20),
        cost_estimate=pl.CostEstimate(flops=5 * 10**9, bytes_accessed=16 * 10**6, transcendentals=0),
        name="update",
    )(place, weights, tile, cov, rows_t)


def row_perm(shift):
    return [(y * 2 + core, ((y + shift) % NY) * 2 + core) for y in range(NY) for core in range(2)]


def x_perm(shift, limit):
    return [(z * NX + x, z * NX + (x + shift) % NX) for z in range(NZ) for x in range(limit)]


def z_perm(step):
    pairs = [(z, z + step) for z in range(0, NZ, 2 * step)]
    return [(a * NX + x, b * NX + x) for a, b in pairs for x in range(PANELS)]


CORES = [(2 * y + core, 2 * y + 1 - core) for y in range(NY) for core in range(2)]


def after(arrays, *done):
    return lax.optimization_barrier((tuple(arrays), done))[0]


def gather_row(block):
    return [block] + [lax.ppermute(block, "row", row_perm(s)) for s in (1, 2, 3)]


def turn_pairs():
    return [(q * 32 + g * 8 + m, m * 32 + g * 8 + (q ^ m)) for q in range(8) for g in range(4) for m in range(8)]


def shards(covariance):
    row = lax.axis_index("row")
    col = lax.axis_index("col")
    place = jnp.stack([row, col]).astype(jnp.int32)
    z_index, x_index = col // NX, col % NX
    top = covariance[0].reshape(NB, 2 * NB)
    cov = covariance.reshape(8, NB, 2, 2, 128).transpose(0, 1, 3, 2, 4).reshape(8, 4 * NB, 128)
    piece = lax.all_to_all(top, "row", 0, 0, tiled=True)[: K // 8]

    turned = lax.ppermute(piece, ("row", "col"), turn_pairs())
    (part,) = after((piece[:, :NB],), place)
    for step in (4, 2, 1):
        got = lax.ppermute(part, "col", z_perm(step))
        part = jnp.where(z_index % (2 * step) == step, got, part)
        if step == 4:
            (turned,) = after((turned,), part)
    rows_t = lax.all_gather(turned, "col", axis=0).reshape(4, K, 2 * NB)

    around = [part] + [lax.ppermute(part, "col", x_perm(s, PANELS)) for s in (1, 2, 3)]
    wide = []
    for q in range(PANELS):
        s = (x_index + NX - q) % NX
        pick = jnp.where(s < 2, jnp.where(s == 0, around[0], around[1]), jnp.where(s == 2, around[2], around[3]))
        wide.append(pick)
    wide = [wide[q][32 * p : 32 * p + 32] for p in range(PANELS) for q in range(p, PANELS)]
    wide = jnp.concatenate(wide + [piece[32 * p : 32 * p + 32] for p in range(PANELS)], axis=1)
    da = jnp.stack(gather_row(wide))
    db = lax.ppermute(da, "row", CORES)

    weights, tile = factor(place, da, db)
    out = update(place, weights, tile, cov, rows_t)
    return out.reshape(8, NB, 2, 2, 128).transpose(0, 1, 3, 2, 4).reshape(8, NB, 2, NB)


def solution(mesh):
    return jax.shard_map(
        shards,
        mesh=mesh,
        in_specs=(P(None, "row", None, "col"),),
        out_specs=P(None, "row", None, "col"),
        check_vma=False,
    )
```

```python
import functools

import jax
import jax.numpy as jnp
from jax import lax
from jax.experimental import pallas as pl
from jax.experimental.pallas import tpu as pltpu
from jax.sharding import PartitionSpec as P

NB = 256
PANELS = 3
K = PANELS * NB
NY, NX, NZ = 4, 4, 8
HI = lax.Precision.HIGHEST
F32 = jnp.float32
BASE = 128
GROUP = 8


def dot(a, b, over):
    return lax.dot_general(a, b, (over, ((), ())), precision=HI, preferred_element_type=F32)


ROWS = ((1,), (0,))
TURN = ((0,), (0,))


def total(terms):
    while len(terms) > 1:
        terms = [terms[i] + terms[i + 1] if i + 1 < len(terms) else terms[i] for i in range(0, len(terms), 2)]
    return terms[0]


def factor_base(block, tasks):
    count = BASE // GROUP
    sub = lax.broadcasted_iota(jnp.int32, (GROUP, BASE), 0)
    lane = lax.broadcasted_iota(jnp.int32, (GROUP, BASE), 1)
    rows = [block[GROUP * h : GROUP * h + GROUP, :] for h in range(count)]

    def spread_row(a, i):
        return jnp.broadcast_to(a[i : i + 1, :], (GROUP, BASE))

    def spread_lane(a, j):
        return jnp.broadcast_to(a[:, j : j + 1], (GROUP, BASE))

    upper, inverse = [], []
    each = -(-len(tasks) // (count - 1))
    for g in range(count):
        lo, hi = GROUP * g, GROUP * g + GROUP
        inside = (lane >= lo) & (lane < hi)
        old = rows[g]
        pivot = [spread_lane(old, lo + j) for j in range(GROUP)]
        v = jnp.where(inside, jnp.where(lane == sub + lo, 1.0, 0.0), old)
        x = jnp.zeros((GROUP, BASE), F32)
        diag = jnp.ones((GROUP, BASE), F32)
        for i in range(GROUP):
            here = sub == i
            d = spread_row(pivot[i], i)
            scale = jnp.where(here, 0.0, pivot[i]) / d
            b = spread_row(v, i)
            x = jnp.where(here, b, x)
            diag = jnp.where(here, d, diag)
            for j in range(i + 1, GROUP):
                pivot[j] = pivot[j] - scale * spread_row(pivot[j], i)
            v = v - scale * b
        z = v / diag
        zs = [spread_row(z, k) for k in range(GROUP)]
        for h in range(g + 1, count):
            terms = [spread_lane(rows[h], lo + k) * zs[k] for k in range(GROUP)]
            rows[h] = jnp.where(inside, 0.0, rows[h]) - total(terms)
        x = x * lax.rsqrt(diag)
        corner = total([spread_lane(x, lo + k) * spread_row(old, k) for k in range(GROUP)])
        upper.append(jnp.where(lane >= hi, x, jnp.where(lane >= lo, corner, 0.0)))
        inverse.append(jnp.where(lane < hi, x, 0.0))
        for _ in range(each):
            if tasks:
                tasks.pop(0)()
    while tasks:
        tasks.pop(0)()
    return jnp.concatenate(upper, 0), jnp.concatenate(inverse, 0)


def factor_all(lt, inv, u, w, col):
    inv[...] = jnp.zeros((K, K), F32)
    w[...] = jnp.zeros((K, 2 * NB), F32)
    in_panel = col < PANELS
    block = lt[:BASE, :BASE]
    tasks = []
    for o in range(0, K, BASE):
        e = o + BASE
        xs, xi = factor_base(block, tasks)
        lt[o:e, o:e] = xs
        inv[o:e, o:e] = xi
        if e < K:
            n = e + BASE
            near = dot(xi, lt[o:e, e:n], ROWS)
            block = lt[e:n, e:n] - dot(near, near, TURN)
            lt[o:e, e:n] = near

        def panel(o=o, e=e, xi=xi):
            if e + BASE < K:
                lt[o:e, e + BASE :] = dot(xi, lt[o:e, e + BASE :], ROWS)

        def solve(o=o, e=e, xi=xi):
            u[o:e, :] = dot(xi, u[o:e, :], ROWS)

        def invert(o=o, e=e, xi=xi):
            if o:
                inv[o:e, :o] = dot(xi, inv[o:e, :o], ROWS)

        def weigh(o=o, e=e):
            sub = lax.broadcasted_iota(jnp.int32, (BASE, NB), 0)
            lane = lax.broadcasted_iota(jnp.int32, (BASE, NB), 1)
            unit = jnp.where(sub + o == lane + col * NB, -1.0, 0.0).astype(F32)
            left = jnp.where(in_panel, unit, u[o:e, :NB])
            right = u[o:e, NB:]
            for c in range(0, e, NB):
                t = min(c + NB, e)
                w[c:t, :NB] = w[c:t, :NB] + dot(inv[o:e, c:t], left, TURN)
                w[c:t, NB:] = w[c:t, NB:] + dot(inv[o:e, c:t], right, TURN)

        def trail(b, o=o, e=e):
            t = b + BASE
            p = lt[o:e, b:t]
            if b > e:
                lt[b:t, b:] = lt[b:t, b:] - dot(p, lt[o:e, b:], TURN)
            elif t < K:
                lt[b:t, t:] = lt[b:t, t:] - dot(p, lt[o:e, t:], TURN)

        def trail_inv(b, o=o, e=e):
            inv[b : b + BASE, :e] = inv[b : b + BASE, :e] - dot(lt[o:e, b : b + BASE], inv[o:e, :e], TURN)

        def trail_u(b, o=o, e=e):
            u[b : b + BASE, :] = u[b : b + BASE, :] - dot(lt[o:e, b : b + BASE], u[o:e, :], TURN)

        later = range(e, K, BASE)
        tasks = [panel] + [functools.partial(trail, b) for b in later] + [invert, solve]
        tasks += [functools.partial(trail_inv, b) for b in later]
        tasks += [functools.partial(trail_u, b) for b in later] + [weigh]
    while tasks:
        tasks.pop(0)()


def factor_kernel(at_ref, da_ref, db_ref, split, tile, lt, inv, u, w):
    row, col = at_ref[0], at_ref[1]
    y_index, core = row // 2, row % 2
    for s in range(NY):
        y_from = (y_index + NY - s) % NY
        for d_from, which in ((da_ref, core), (db_ref, 1 - core)):
            at = 32 * (2 * y_from + which)
            lane = 0
            for p in range(PANELS):
                place = pl.ds(pl.multiple_of(p * NB + at, 32), 32)
                wide = K - p * NB
                lt[place, p * NB :] = d_from[s, :, lane : lane + wide]
                lane += wide
            for p in range(PANELS):
                place = pl.ds(pl.multiple_of(p * NB + at, 32), 32)
                u[place, :] = d_from[s, :, lane : lane + 2 * NB]
                lane += 2 * NB
    factor_all(lt, inv, u, w, col)

    for j in range(PANELS):
        o, e = j * NB, (j + 1) * NB
        hi = w[o:e, :].astype(jnp.bfloat16)
        lo = (w[o:e, :] - hi.astype(F32)).astype(jnp.bfloat16)
        for r in range(8):
            to = pl.ds(pl.multiple_of((r ^ row) * 96 + j * 32, 32), 32)
            split[to, : 2 * NB] = hi[r * 32 : r * 32 + 32, :]
            split[to, 2 * NB :] = lo[r * 32 : r * 32 + 32, :]
    tile[...] = jnp.zeros((NB, NB), F32)

    @pl.when((col < PANELS) & (row < PANELS) & (row >= col))
    def _():
        p_row = pl.multiple_of(row * NB, NB)
        p_col = pl.multiple_of(col * NB, NB)
        part = lt[pl.ds(p_col, NB), pl.ds(p_row, NB)]
        sub = lax.broadcasted_iota(jnp.int32, (NB, NB), 0)
        lane = lax.broadcasted_iota(jnp.int32, (NB, NB), 1)
        tile[...] = jnp.where((row > col) | (lane >= sub), part, 0.0).T


def factor(place, da, db):
    vmem = pl.BlockSpec(memory_space=pltpu.VMEM)
    return pl.pallas_call(
        factor_kernel,
        in_specs=[pl.BlockSpec(memory_space=pltpu.SMEM), vmem, vmem],
        out_specs=[vmem] * 2,
        out_shape=[
            jax.ShapeDtypeStruct((K, 4 * NB), jnp.bfloat16),
            jax.ShapeDtypeStruct((NB, NB), F32),
        ],
        scratch_shapes=[
            pltpu.VMEM((K, K), F32),
            pltpu.VMEM((K, K), F32),
            pltpu.VMEM((K, 2 * NB), F32),
            pltpu.VMEM((K, 2 * NB), F32),
        ],
        compiler_params=pltpu.CompilerParams(vmem_limit_bytes=28 * 2**20),
        cost_estimate=pl.CostEstimate(flops=4 * 10**9, bytes_accessed=10**7, transcendentals=0),
        name="factor",
    )(place, da, db)


def update_kernel(at_ref, split, tile, cov_ref, rows_ref, out_ref, buf, acc, in_sem, cov_sem, out_sem):
    row, col = at_ref[0], at_ref[1]

    def load(k):
        lanes = pl.ds(pl.multiple_of(k // 4 * NB, NB), NB)
        return pltpu.make_async_copy(rows_ref.at[k % 4, :, lanes], buf.at[k], in_sem.at[k])

    def base(k):
        return pltpu.make_async_copy(cov_ref.at[k], acc.at[k], cov_sem.at[k])

    def store(k):
        return pltpu.make_async_copy(acc.at[k], out_ref.at[k], out_sem.at[k])

    def fetch(k):
        load(k).start()
        base(k).start()

    fetch(0)
    fetch(1)

    def step(k, carry):
        load(k).wait()
        base(k).wait()

        @pl.when(k < 6)
        def _():
            fetch(k + 2)

        over = (TURN, ((), ()))
        rows = buf[k]
        hi = rows.astype(jnp.bfloat16)
        lo = (rows - hi.astype(F32)).astype(jnp.bfloat16)
        both = lax.dot_general(hi, split[...], over, preferred_element_type=F32)
        small = lax.dot_general(lo, split[:, : 2 * NB], over, preferred_element_type=F32)
        product = both[:, : 2 * NB] + (both[:, 2 * NB :] + small)
        for q in range(4):
            place = pl.ds(q, NB, stride=4)
            at = (q % 2) * NB + (q // 2) * 128
            left = acc[k, place, :]
            if q % 2 == 0:
                left = jnp.where(col < PANELS, 0.0, left)
            acc[k, place, :] = left - product[:, at : at + 128]

        @pl.when((k == 0) & (row < PANELS))
        def _():
            for part in range(2):
                acc[0, pl.ds(2 * part, NB, stride=4), :] = tile[:, part * 128 : part * 128 + 128]
                acc[0, pl.ds(2 * part + 1, NB, stride=4), :] = jnp.zeros((NB, 128), F32)

        store(k).start()
        return carry

    lax.fori_loop(0, 8, step, 0)
    for k in range(8):
        store(k).wait()


def update(place, weights, tile, cov, rows_t):
    vmem = pl.BlockSpec(memory_space=pltpu.VMEM)
    hbm = pl.BlockSpec(memory_space=pltpu.HBM)
    return pl.pallas_call(
        update_kernel,
        in_specs=[pl.BlockSpec(memory_space=pltpu.SMEM), vmem, vmem, hbm, hbm],
        out_specs=hbm,
        out_shape=jax.ShapeDtypeStruct((8, 4 * NB, 128), F32),
        scratch_shapes=[
            pltpu.VMEM((8, K, NB), F32),
            pltpu.VMEM((8, 4 * NB, 128), F32),
            pltpu.SemaphoreType.DMA((8,)),
            pltpu.SemaphoreType.DMA((8,)),
            pltpu.SemaphoreType.DMA((8,)),
        ],
        compiler_params=pltpu.CompilerParams(vmem_limit_bytes=50 * 2**20),
        cost_estimate=pl.CostEstimate(flops=5 * 10**9, bytes_accessed=16 * 10**6, transcendentals=0),
        name="update",
    )(place, weights, tile, cov, rows_t)


def row_perm(shift):
    return [(y * 2 + core, ((y + shift) % NY) * 2 + core) for y in range(NY) for core in range(2)]


def x_perm(shift, limit):
    return [(z * NX + x, z * NX + (x + shift) % NX) for z in range(NZ) for x in range(limit)]


def z_perm(step):
    pairs = [(z, z + step) for z in range(0, NZ, 2 * step)]
    return [(a * NX + x, b * NX + x) for a, b in pairs for x in range(PANELS)]


CORES = [(2 * y + core, 2 * y + 1 - core) for y in range(NY) for core in range(2)]


def after(arrays, *done):
    return lax.optimization_barrier((tuple(arrays), done))[0]


def gather_row(block):
    return [block] + [lax.ppermute(block, "row", row_perm(s)) for s in (1, 2, 3)]


def turn_pairs():
    return [(q * 32 + g * 8 + m, m * 32 + g * 8 + (q ^ m)) for q in range(8) for g in range(4) for m in range(8)]


def shards(covariance):
    row = lax.axis_index("row")
    col = lax.axis_index("col")
    place = jnp.stack([row, col]).astype(jnp.int32)
    z_index, x_index = col // NX, col % NX
    top = covariance[0].reshape(NB, 2 * NB)
    cov = covariance.reshape(8, NB, 2, 2, 128).transpose(0, 1, 3, 2, 4).reshape(8, 4 * NB, 128)
    piece = lax.all_to_all(top, "row", 0, 0, tiled=True)[: K // 8]

    turned = lax.ppermute(piece, ("row", "col"), turn_pairs())
    (part,) = after((piece[:, :NB],), place)
    for step in (4, 2, 1):
        got = lax.ppermute(part, "col", z_perm(step))
        part = jnp.where(z_index % (2 * step) == step, got, part)
        if step == 4:
            (turned,) = after((turned,), part)
    rows_t = lax.all_gather(turned, "col", axis=0).reshape(4, K, 2 * NB)

    around = [part] + [lax.ppermute(part, "col", x_perm(s, PANELS)) for s in (1, 2, 3)]
    wide = []
    for q in range(PANELS):
        s = (x_index + NX - q) % NX
        pick = jnp.where(s < 2, jnp.where(s == 0, around[0], around[1]), jnp.where(s == 2, around[2], around[3]))
        wide.append(pick)
    wide = [wide[q][32 * p : 32 * p + 32] for p in range(PANELS) for q in range(p, PANELS)]
    wide = jnp.concatenate(wide + [piece[32 * p : 32 * p + 32] for p in range(PANELS)], axis=1)
    da = jnp.stack(gather_row(wide))
    db = lax.ppermute(da, "row", CORES)

    weights, tile = factor(place, da, db)
    out = update(place, weights, tile, cov, rows_t)
    return out.reshape(8, NB, 2, 2, 128).transpose(0, 1, 3, 2, 4).reshape(8, NB, 2, NB)


def solution(mesh):
    return jax.shard_map(
        shards,
        mesh=mesh,
        in_specs=(P(None, "row", None, "col"),),
        out_specs=P(None, "row", None, "col"),
        check_vma=False,
    )
```
